256 devices in a mesh: dp: 4 (over y), bank: 64 (over z, x, core).
Axes of the slice: x: 4, y: 4, z: 8, core: 2. Of those that a mesh axis runs over, the one named last changes fastest.
Arguments:
- region_codes: bfloat16 [2048, 1024], P(('dp', 'bank')), parts along dimension 0
- block_exponents: int32 [2048, 32], P(('dp', 'bank')), parts along dimension 0, may hold values from -3 to 2
- text_bank: bfloat16 [262144, 1024], P('bank')
Outputs:
- expected: bfloat16 [2048, 1024], P(('dp', 'bank')), parts along dimension 0
The draws below stay inside these ranges and needn't reach their ends.
There are 4 independent parts, one for each index of `dp`. The reference program is written for one: setup_inputs(seed, part) draws one part's arguments, and reference() takes and returns one part's arrays. A program takes and returns all parts, laid end to end along the dimension named above; an argument that names none is the same for every part. Nothing has to cross between parts.
All inputs are finite; a program needn't handle non-finite values.
Results may differ from the reference program's by a relative error of at most 0.003.
Values may be sent and summed in bfloat16 or wider, within the bound.
A program may use at most 320 MiB of HBM per device.

```python
import math
import jax
import jax.numpy as jnp
from jax import lax

D = 1024
REGIONS = 512
VDEV = 4096
CONCEPTS = 262144
N_BANK = 64


def draw_exponent_table(key):
    return jax.random.randint(jax.random.fold_in(key, 7), (REGIONS, D // 32), -3, 3)


def draw_block_exponents(key, part):
    exponents = draw_exponent_table(key)
    return exponents.astype(jnp.int32)


def draw_text_bank(key, part):
    key = jax.random.fold_in(key, 3)
    concept_base = jax.random.normal(key, (CONCEPTS, D), jnp.float32) / math.sqrt(D)
    return concept_base.astype(jnp.bfloat16)


def draw_region_codes(key, part):
    key = jax.random.fold_in(key, 5)
    values = jax.random.normal(key, (REGIONS, D), jnp.float32)
    return values.astype(jnp.bfloat16)


def setup_inputs(seed: int = 0, part: int = 0) -> dict:
    splits = jax.random.split(jax.random.key(seed), 4)
    part_keys = jax.random.split(jax.random.fold_in(splits[3], part), 4)
    return {
        "region_codes": draw_region_codes(jax.random.fold_in(jax.random.fold_in(splits[3], part), 71), part),
        "block_exponents": draw_block_exponents(jax.random.fold_in(jax.random.fold_in(splits[3], part), 71), part),
        "text_bank": draw_text_bank(jax.random.fold_in(splits[3], 71), part),
    }


logit_scale = 2.0


def dequantize(codes, exponents):
    expanded = jnp.repeat(jnp.exp2(exponents.astype(jnp.float32)), 32, axis=1)
    return (codes.astype(jnp.float32) * expanded).astype(jnp.bfloat16)


def reference(region_codes, block_exponents, text_bank):
    regions = dequantize(region_codes, block_exponents)
    blocks = text_bank.reshape(N_BANK, VDEV, D)

    def score_block(block):
        logits = logit_scale * lax.dot_general(regions, block, (((1,), (1,)), ((), ())), preferred_element_type=jnp.float32)
        peaks = jnp.max(logits, axis=1)
        shifted = jnp.exp(logits - peaks[:, None])
        totals = jnp.sum(shifted, axis=1)
        partial_value = jnp.dot(shifted.astype(jnp.bfloat16), block, preferred_element_type=jnp.float32)
        return peaks, totals, partial_value

    peaks, totals, partial_value = lax.map(score_block, blocks)
    highest = jnp.max(peaks, axis=0)
    factor = jnp.exp(peaks - highest[None, :])
    numerator = jnp.sum(partial_value * factor[:, :, None], axis=0)
    denominator = jnp.sum(totals * factor, axis=0)
    return (numerator / denominator[:, None]).astype(jnp.bfloat16)
```

```python
import math

import jax
import jax.numpy as jnp
from jax import lax
from jax.experimental import pallas as pl
from jax.experimental.pallas import tpu as pltpu
from jax.sharding import PartitionSpec as P

MESH = pl.DeviceIdType.MESH
D = 1024
HALF = D // 2
VDEV = 4096
NZ, NX = 8, 4
OWN = 8
PLANE = 2 * NX * OWN
WIDE = D + 128
SLOTS = (0, 1, 7, 2, 6, 3, 5, 4)
FAR = (4, 3, 5, 2, 6, 1, 7)
CHUNK = 2 * PLANE
NCHUNK = NZ // 2
LOADS = 8
QTILE = 1024
SCALE = 2.0 / math.log(2.0)


def merge(parts):
    top = parts[0][0]
    for m, _, _ in parts[1:]:
        top = jnp.maximum(top, m)
    total, rows = None, None
    for m, s, p in parts:
        f = jnp.exp2((m - top) * SCALE)
        total = s * f if total is None else total + s * f
        rows = p * f if rows is None else rows + p * f
    return top, total, rows


def pack_ms(m, s):
    lane = lax.broadcasted_iota(jnp.int32, (m.shape[0], 128), 1)
    return jnp.where(lane < 64, m, s)


def unpack_ms(tile):
    return tile[:, 0:1], tile[:, 64:65]


def to_travel(rows):
    return jnp.concatenate([rows[:, :HALF], rows[:, HALF:]], axis=0)


def from_travel(block):
    return jnp.concatenate([block[:OWN], block[OWN:]], axis=1)


def kernel(
    codes_ref, exps_ref, text_hbm, out_ref,
    text, gath, regs, logit, wgt, pbuf, cbuf, xsend, xsms, xb, xbms, qown, zsend, zb,
    load_sem, gz_s, gz_r, gx_s, gx_r, gc_s, gc_r, rc_s, rc_r, rx_s, rx_r, rm_s, rm_r, rz_s, rz_r,
):
    me = lax.axis_index("bank")
    z, x, c = me // (2 * NX), (me // 2) % NX, me % 2

    def at(dz, dx, dc):
        return {"bank": ((z + dz) % NZ) * (2 * NX) + ((x + dx) % NX) * 2 + (c + dc) % 2}

    def remote(src, dst, s, r, dev):
        return pltpu.make_async_remote_copy(
            src_ref=src, dst_ref=dst, send_sem=s, recv_sem=r, device_id=dev, device_id_type=MESH
        )

    span = VDEV // LOADS
    loads = [
        pltpu.make_async_copy(
            text_hbm.at[pl.ds(k * span, span)], text.at[pl.ds(k * span, span)], load_sem.at[k]
        )
        for k in range(LOADS)
    ]
    for ld in loads:
        ld.start()

    scale = jnp.exp2(exps_ref[...].astype(jnp.float32)).astype(jnp.bfloat16)
    feat = lax.broadcasted_iota(jnp.int32, (32, D), 1) // 32
    blk = lax.broadcasted_iota(jnp.int32, (32, D), 0)
    spread = jnp.where(feat == blk, 1.0, 0.0).astype(jnp.bfloat16)
    expanded = jnp.dot(scale, spread, preferred_element_type=jnp.float32)
    own = codes_ref[...].astype(jnp.float32) * expanded
    gath[0, 0, 0] = to_travel(own).astype(jnp.bfloat16)

    barrier = pltpu.get_barrier_semaphore()
    peers = [at(d, 0, 0) for d in FAR] + [at(0, i, 0) for i in (2, 1, 3)] + [at(0, 0, 1)]
    for p in peers:
        pl.semaphore_signal(barrier, inc=1, device_id=p, device_id_type=MESH)
    pl.semaphore_wait(barrier, len(peers))

    started = []

    def go(copy):
        copy.start()
        started.append(copy)
        return copy

    gz = {}
    for e in FAR:
        d = (NZ - e) % NZ
        gz[d] = go(remote(gath.at[0, 0, 0], gath.at[d, 0, 0], gz_s.at[d], gz_r.at[d], at(e, 0, 0)))
    gx = {}

    def forward(d):
        for i in (2, 1, 3):
            j = NX - i
            gx[d, j] = go(remote(gath.at[d, 0, 0], gath.at[d, 0, j], gx_s.at[d, j], gx_r.at[d, j], at(0, i, 0)))

    gc = {}

    def swap(d):
        for j in (1, 2, 3):
            gx[d, j].wait_recv()
        gc[d] = go(remote(gath.at[d, 0], gath.at[d, 1], gc_s.at[d], gc_r.at[d], at(0, 0, 1)))

    forward(0)
    for d in SLOTS[1:]:
        gz[d].wait_recv()
        forward(d)
    for slot, d in enumerate(SLOTS):
        swap(d)
    for slot, d in enumerate(SLOTS):
        gc[d].wait_recv()
        for cr in range(2):
            for i in range(0, NX, 2):
                a = from_travel(gath[d, cr, i].astype(jnp.float32))
                b = from_travel(gath[d, cr, i + 1].astype(jnp.float32))
                r0 = slot * PLANE + cr * (NX * OWN) + i * OWN
                regs[r0 : r0 + 2 * OWN, :] = jnp.concatenate([a, b], axis=0).astype(jnp.bfloat16)
    for ld in loads:
        ld.wait()

    n = NZ * PLANE
    peak = jnp.full((n, 128), -jnp.inf, jnp.float32)
    for t in range(VDEV // QTILE):
        dots = lax.dot_general(
            regs[...], text[t * QTILE : (t + 1) * QTILE, :], (((1,), (1,)), ((), ())),
            preferred_element_type=jnp.float32,
        )
        logit[:, t * QTILE : (t + 1) * QTILE] = dots
        for q in range(QTILE // 128):
            peak = jnp.maximum(peak, dots[:, q * 128 : (q + 1) * 128])
    top = jnp.max(peak, axis=1, keepdims=True)

    rc, rx, rm, rz = {}, {}, {}, {}
    order = list(range(NCHUNK - 1, -1, -1))

    def weights(g):
        lo = g * CHUNK
        m = top[lo : lo + CHUNK]
        total = jnp.zeros((CHUNK, 128), jnp.float32)
        for k in range(VDEV // 128):
            e = jnp.exp2((logit[lo : lo + CHUNK, k * 128 : (k + 1) * 128] - m) * SCALE)
            total = total + e
            wgt[lo : lo + CHUNK, k * 128 : (k + 1) * 128] = e.astype(jnp.bfloat16)
        s = jnp.sum(total, axis=1, keepdims=True)
        pbuf[lo : lo + CHUNK, D:] = pack_ms(m, s)

    def values(g):
        lo = g * CHUNK
        for k in range(2):
            pbuf[lo : lo + CHUNK, k * HALF : (k + 1) * HALF] = jnp.dot(
                wgt[lo : lo + CHUNK, :], text[:, k * HALF : (k + 1) * HALF], preferred_element_type=jnp.float32
            )
        for slot in (2 * g + 1, 2 * g):
            rc[slot] = go(remote(
                pbuf.at[pl.ds(slot * PLANE + NX * OWN, NX * OWN)], cbuf.at[slot],
                rc_s.at[slot], rc_r.at[slot], at(0, 0, 1),
            ))

    def pair_sum(slot):
        rc[slot].wait_recv()
        lo = slot * PLANE
        a = pbuf[lo : lo + NX * OWN, :]
        b = cbuf[slot]
        m, s, p = merge([(*unpack_ms(a[:, D:]), a[:, :D]), (*unpack_ms(b[:, D:]), b[:, :D])])
        ms = pack_ms(m, s)
        qown[slot, :, :D] = p[:OWN]
        qown[slot, :, D:] = ms[:OWN]
        for i in (2, 1, 3):
            j = NX - i
            xsend[slot, i] = to_travel(p[i * OWN : (i + 1) * OWN]).astype(jnp.bfloat16)
            xsms[slot, i] = ms[i * OWN : (i + 1) * OWN]
            rx[slot, j] = go(remote(xsend.at[slot, i], xb.at[slot, j], rx_s.at[slot, i], rx_r.at[slot, j], at(0, i, 0)))
            rm[slot, j] = go(remote(xsms.at[slot, i], xbms.at[slot, j], rm_s.at[slot, i], rm_r.at[slot, j], at(0, i, 0)))

    def x_sum(slot):
        d = SLOTS[slot]
        own_part = qown[slot]
        parts = [(*unpack_ms(own_part[:, D:]), own_part[:, :D])]
        for j in (1, 2, 3):
            rx[slot, j].wait_recv()
            rm[slot, j].wait_recv()
            parts.append((*unpack_ms(xbms[slot, j]), from_travel(xb[slot, j].astype(jnp.float32))))
        m, s, p = merge(parts)
        if d == 0:
            zb[0, :, :D] = p
            zb[0, :, D:] = pack_ms(m, s)
            return
        zsend[slot, :, :D] = p
        zsend[slot, :, D:] = pack_ms(m, s)
        e = (NZ - d) % NZ
        rz[e] = go(remote(zsend.at[slot], zb.at[e], rz_s.at[e], rz_r.at[e], at(d, 0, 0)))

    weights(order[0])
    for n_, g in enumerate(order):
        values(g)
        if n_ + 1 < NCHUNK:
            weights(order[n_ + 1])
        if n_ >= 2:
            for slot in (2 * order[n_ - 2] + 1, 2 * order[n_ - 2]):
                x_sum(slot)
        if n_ >= 1:
            for slot in (2 * order[n_ - 1] + 1, 2 * order[n_ - 1]):
                pair_sum(slot)
    last = order[-1]
    for slot in (2 * last + 1, 2 * last):
        pair_sum(slot)
    for g in order[-2:]:
        for slot in (2 * g + 1, 2 * g):
            x_sum(slot)

    parts = []
    for d in range(NZ):
        if d:
            rz[d].wait_recv()
        parts.append((*unpack_ms(zb[d, :, D:]), zb[d, :, :D]))
    m, s, p = merge(parts)
    out_ref[...] = (p / s).astype(jnp.bfloat16)
    for cp in started:
        cp.wait_send()


def local(codes, exps, text_bank):
    dma = pltpu.SemaphoreType.DMA
    f32, bf16 = jnp.float32, jnp.bfloat16
    n = NZ * PLANE
    return pl.pallas_call(
        kernel,
        out_shape=jax.ShapeDtypeStruct((OWN, D), bf16),
        in_specs=[
            pl.BlockSpec(memory_space=pltpu.VMEM),
            pl.BlockSpec(memory_space=pltpu.VMEM),
            pl.BlockSpec(memory_space=pl.ANY),
        ],
        out_specs=pl.BlockSpec(memory_space=pltpu.VMEM),
        scratch_shapes=[
            pltpu.VMEM((VDEV, D), bf16),
            pltpu.VMEM((NZ, 2, NX, 2 * OWN, HALF), bf16),
            pltpu.VMEM((n, D), bf16),
            pltpu.VMEM((n, VDEV), f32),
            pltpu.VMEM((n, VDEV), bf16),
            pltpu.VMEM((n, WIDE), f32),
            pltpu.VMEM((NZ, NX * OWN, WIDE), f32),
            pltpu.VMEM((NZ, NX, 2 * OWN, HALF), bf16),
            pltpu.VMEM((NZ, NX, OWN, 128), f32),
            pltpu.VMEM((NZ, NX, 2 * OWN, HALF), bf16),
            pltpu.VMEM((NZ, NX, OWN, 128), f32),
            pltpu.VMEM((NZ, OWN, WIDE), f32),
            pltpu.VMEM((NZ, OWN, WIDE), f32),
            pltpu.VMEM((NZ, OWN, WIDE), f32),
            dma((LOADS,)),
            dma((NZ,)), dma((NZ,)),
            dma((NZ, NX)), dma((NZ, NX)),
            dma((NZ,)), dma((NZ,)),
            dma((NZ,)), dma((NZ,)),
            dma((NZ, NX)), dma((NZ, NX)),
            dma((NZ, NX)), dma((NZ, NX)),
            dma((NZ,)), dma((NZ,)),
        ],
        compiler_params=pltpu.CompilerParams(
            collective_id=0, has_side_effects=True, vmem_limit_bytes=48 * 2**20
        ),
    )(codes, exps, text_bank)


def solution(mesh):
    return jax.shard_map(
        local,
        mesh=mesh,
        in_specs=(P(("dp", "bank"), None), P(("dp", "bank"), None), P("bank", None)),
        out_specs=P(("dp", "bank"), None),
        check_vma=False,
    )
```

```python
import math

import jax
import jax.numpy as jnp
from jax import lax
from jax.experimental import pallas as pl
from jax.experimental.pallas import tpu as pltpu
from jax.sharding import PartitionSpec as P

MESH = pl.DeviceIdType.MESH
D = 1024
HALF = D // 2
VDEV = 4096
NZ, NX = 8, 4
OWN = 8
PAIR = NX * OWN
PLANE = 2 * PAIR
WIDE = D + 128
MSG = HALF + 128
SLOTS = (0, 1, 7, 2, 6, 3, 5, 4)
CHUNK = 2 * PLANE
NCHUNK = NZ // 2
LOADS = 8
QTILE = 512
DIRECT_IN = (0, 1, 7)
DIRECT_OUT = (0, 1, 7)
BUNDLE_IN = (2, 6)
SENDS = (
    (0, 2), (0, 1), (0, 3), (4, 0), (3, 0), (5, 0), (1, 2), (1, 1), (1, 3), (1, 0), (7, 2), (7, 1), (7, 3), (7,
    0),
)
STEPS = (
    ("t", 0), ("t", 1), ("t", 2), ("t", 3), ("t", 4), ("t", 5), ("t", 6), ("t", 7), ("swap", 0), ("bundle", 2),
    ("bundle", 6), ("fwd", 3), ("fwd", 5), ("fwd", 4), ("swap", 1), ("swap", 7), ("pack", 0), ("pack", 1), ("q",
    0), ("swap", 3), ("swap", 5), ("swap", 4), ("swap", 2), ("swap", 6), ("pack", 6), ("pack", 7), ("q", 3),
    ("w", 0), ("pack", 4), ("pack", 5), ("q", 2), ("w", 3), ("v", 3), ("w", 2), ("give", 3), ("pack", 2),
    ("pack", 3), ("q", 1), ("v", 2), ("w", 1), ("give", 2), ("pair", 7), ("pair", 6), ("v", 1), ("give", 1),
    ("pair", 5), ("pair", 4), ("v", 0), ("give", 0), ("x", 7), ("x", 6), ("pair", 3), ("pair", 2), ("x", 5),
    ("x", 4), ("pair", 1), ("pair", 0), ("x", 3), ("end", 0), ("end", 1), ("end", 7), ("end", 6), ("end", 2),
    ("end", 3), ("end", 5), ("end", 4),
)
SCALE = 2.0 / math.log(2.0)


def merge(parts):
    top = parts[0][0]
    for m, _, _ in parts[1:]:
        top = jnp.maximum(top, m)
    total, rows = None, None
    for m, s, p in parts:
        f = jnp.exp2((m - top) * SCALE)
        total = s * f if total is None else total + s * f
        rows = p * f if rows is None else rows + p * f
    return top, total, rows


def pack_ms(m, s):
    lane = lax.broadcasted_iota(jnp.int32, (m.shape[0], 128), 1)
    return jnp.where(lane < 64, m, s)


def unpack(wide):
    return wide[:, D : D + 1], wide[:, D + 64 : D + 65], wide[:, :D]


def to_travel(rows):
    return jnp.concatenate([rows[:, :HALF], rows[:, HALF:]], axis=0)


def from_travel(block):
    return jnp.concatenate([block[:OWN], block[OWN:]], axis=1)


def to_message(m, s, rows):
    col = jnp.broadcast_to(jnp.concatenate([m, s], axis=0), (2 * OWN, 128))
    hi = col.astype(jnp.bfloat16).astype(jnp.float32)
    mid = (col - hi).astype(jnp.bfloat16).astype(jnp.float32)
    low = (col - hi) - mid
    lane = lax.broadcasted_iota(jnp.int32, col.shape, 1)
    tail = jnp.where(lane < 32, hi, jnp.where(lane < 64, mid, low))
    return jnp.concatenate([to_travel(rows), tail], axis=1).astype(jnp.bfloat16)


def from_message(block):
    wide = block.astype(jnp.float32)
    tail = wide[:, HALF:]
    col = (tail[:, 0:1] + tail[:, 32:33]) + tail[:, 64:65]
    return col[:OWN], col[OWN:], from_travel(wide[:, :HALF])


def kernel(
    codes_hbm, exps_hbm, text_hbm, out_ref,
    codes, exps, text, textt, gath, regs, logit, wgt, pbuf, cbuf, xsend, xb, qown, zsend, zb,
    load_sem, in_sem, gx_s, gx_r, gc_s, gc_r, rc_s, rc_r, rx_s, rx_r, rz_s, rz_r,
):
    me = lax.axis_index("bank")
    z, x, c = me // (2 * NX), (me // 2) % NX, me % 2

    def at(dz, dx, dc):
        return {"bank": ((z + dz) % NZ) * (2 * NX) + ((x + dx) % NX) * 2 + (c + dc) % 2}

    def remote(src, dst, s, r, dev):
        return pltpu.make_async_remote_copy(
            src_ref=src, dst_ref=dst, send_sem=s, recv_sem=r, device_id=dev, device_id_type=MESH
        )

    barrier = pltpu.get_barrier_semaphore()
    far = [(d, 0, 0) for d in (4, 3, 5, 2, 6)]
    near = [(d, i, 0) for d in sorted((set(DIRECT_IN) | set(DIRECT_OUT)) - {0}) for i in range(1, NX)]
    peers = far + near + [(1, 0, 0), (7, 0, 0), (0, 2, 0), (0, 1, 0), (0, 3, 0), (0, 0, 1)]
    for p in peers:
        pl.semaphore_signal(barrier, inc=1, device_id=at(*p), device_id_type=MESH)

    in_codes = pltpu.make_async_copy(codes_hbm, codes, in_sem.at[0])
    in_exps = pltpu.make_async_copy(exps_hbm, exps, in_sem.at[1])
    in_codes.start()
    in_exps.start()
    span = VDEV // LOADS
    loads = [
        pltpu.make_async_copy(
            text_hbm.at[pl.ds(k * span, span)], text.at[pl.ds(k * span, span)], load_sem.at[k]
        )
        for k in range(LOADS)
    ]
    for ld in loads:
        ld.start()

    feat = lax.broadcasted_iota(jnp.int32, (32, D), 1) // 32
    blk = lax.broadcasted_iota(jnp.int32, (32, D), 0)
    spread = jnp.where(feat == blk, 1.0, 0.0).astype(jnp.bfloat16)
    in_codes.wait()
    in_exps.wait()
    scale = jnp.exp2(exps[...].astype(jnp.float32)).astype(jnp.bfloat16)
    expanded = jnp.dot(scale, spread, preferred_element_type=jnp.float32)
    own = codes[...].astype(jnp.float32) * expanded
    gath[0, 0, 0] = to_travel(own).astype(jnp.bfloat16)
    pl.semaphore_wait(barrier, len(peers))

    started = []

    def go(copy):
        copy.start()
        started.append(copy)
        return copy

    gx, gc = {}, {}

    def send(e, i):
        d, j = (NZ - e) % NZ, (NX - i) % NX
        gx[d, j] = go(remote(gath.at[0, 0, 0], gath.at[d, 0, j], gx_s.at[d, j], gx_r.at[d, j], at(e, i, 0)))

    def forward(d):
        gx[d, 0].wait_recv()
        for i in (2, 1, 3):
            j = NX - i
            gx[d, j] = go(remote(gath.at[d, 0, 0], gath.at[d, 0, j], gx_s.at[d, j], gx_r.at[d, j], at(0, i, 0)))

    def bundle(e):
        d = (NZ - e) % NZ
        gx[d, 0] = go(remote(gath.at[0, 0], gath.at[d, 0], gx_s.at[d, 0], gx_r.at[d, 0], at(e, 0, 0)))

    def swap(d):
        if d in BUNDLE_IN:
            gx[d, 0].wait_recv()
        else:
            for j in range(NX):
                if j or (d and d in DIRECT_IN):
                    gx[d, j].wait_recv()
        gc[d] = go(remote(gath.at[d, 0], gath.at[d, 1], gc_s.at[d], gc_r.at[d], at(0, 0, 1)))

    def transpose(k):
        loads[k].wait()
        textt[:, k * span : (k + 1) * span] = text[k * span : (k + 1) * span, :].T

    def repack(slot):
        d = SLOTS[slot]
        gc[d].wait_recv()
        for cr in range(2):
            for i in range(0, NX, 2):
                a = from_travel(gath[d, cr, i].astype(jnp.float32))
                b = from_travel(gath[d, cr, i + 1].astype(jnp.float32))
                r0 = slot * PLANE + cr * PAIR + i * OWN
                regs[r0 : r0 + 2 * OWN, :] = jnp.concatenate([a, b], axis=0).astype(jnp.bfloat16)

    top = {}

    def logits(g):
        lo = g * CHUNK
        peak = jnp.full((CHUNK, 128), -jnp.inf, jnp.float32)
        for t in range(VDEV // QTILE):
            dots = jnp.dot(
                regs[lo : lo + CHUNK, :], textt[:, t * QTILE : (t + 1) * QTILE],
                preferred_element_type=jnp.float32,
            )
            logit[g, :, t * QTILE : (t + 1) * QTILE] = dots
            for q in range(QTILE // 128):
                peak = jnp.maximum(peak, dots[:, q * 128 : (q + 1) * 128])
        top[g] = jnp.max(peak, axis=1, keepdims=True)

    def weights(g):
        lo = g * CHUNK
        total = jnp.zeros((CHUNK, 128), jnp.float32)
        for k in range(VDEV // 128):
            e = jnp.exp2((logit[g, :, k * 128 : (k + 1) * 128] - top[g]) * SCALE)
            total = total + e
            wgt[lo : lo + CHUNK, k * 128 : (k + 1) * 128] = e.astype(jnp.bfloat16)
        s = jnp.sum(total, axis=1, keepdims=True)
        pbuf[lo : lo + CHUNK, D:] = pack_ms(top[g], s)

    rc, rx, rz = {}, {}, {}

    def values(g):
        lo = g * CHUNK
        for k in range(2):
            pbuf[lo : lo + CHUNK, k * HALF : (k + 1) * HALF] = jnp.dot(
                wgt[lo : lo + CHUNK, :], text[:, k * HALF : (k + 1) * HALF], preferred_element_type=jnp.float32
            )
            if k == 0:
                give(g, 0)

    def give(g, k=1):
        cols = pl.ds(0, HALF) if k == 0 else pl.ds(HALF, WIDE - HALF)
        for slot in (2 * g + 1, 2 * g):
            rc[slot, k] = go(remote(
                pbuf.at[pl.ds(slot * PLANE + PAIR, PAIR), cols], cbuf.at[slot, :, cols],
                rc_s.at[slot, k], rc_r.at[slot, k], at(0, 0, 1),
            ))

    def pair_sum(slot):
        d = SLOTS[slot]
        rc[slot, 0].wait_recv()
        rc[slot, 1].wait_recv()
        lo = slot * PLANE
        m, s, p = merge([unpack(pbuf[lo : lo + PAIR, :]), unpack(cbuf[slot])])
        straight = d in DIRECT_OUT
        e = (NZ - d) % NZ if straight else d
        for i in (2, 1, 3, 0):
            j = (NX - i) % NX
            lo, hi = i * OWN, (i + 1) * OWN
            if i == 0 and not (straight and d):
                qown[slot, :, :D] = p[lo:hi]
                qown[slot, :, D:] = pack_ms(m[lo:hi], s[lo:hi])
                continue
            xsend[d, i] = to_message(m[lo:hi], s[lo:hi], p[lo:hi])
            rx[e, j] = go(remote(
                xsend.at[d, i], xb.at[e, j], rx_s.at[d, i], rx_r.at[e, j], at(d if straight else 0, i, 0)
            ))

    def plane(e, first):
        parts = list(first)
        for j in range(NX):
            if j or not first:
                rx[e, j].wait_recv()
                parts.append(from_message(xb[e, j]))
        return parts

    def x_sum(slot):
        d = SLOTS[slot]
        m, s, p = merge(plane(d, [unpack(qown[slot])]))
        zsend[d] = to_message(m, s, p)
        e = (NZ - d) % NZ
        rz[e] = go(remote(zsend.at[d], zb.at[e], rz_s.at[e], rz_r.at[e], at(d, 0, 0)))

    result = []

    def collect(e):
        if e == 0:
            parts = plane(0, [unpack(qown[0])])
        elif e in DIRECT_OUT:
            parts = plane(e, [])
        else:
            rz[e].wait_recv()
            parts = [from_message(zb[e])]
        result[:] = [merge(result + parts)]

    run = {
        "t": transpose, "fwd": forward, "bundle": bundle, "swap": swap, "pack": repack, "q": logits, "w": weights, "v": values,
        "give": give, "pair": pair_sum, "x": x_sum, "end": collect,
    }
    for e, i in SENDS:
        send(e, i)
    for name, k in STEPS:
        run[name](k)
    m, s, p = result[0]
    out_ref[...] = (p / s).astype(jnp.bfloat16)
    for cp in started:
        cp.wait_send()


def local(codes, exps, text_bank):
    dma = pltpu.SemaphoreType.DMA
    f32, bf16 = jnp.float32, jnp.bfloat16
    n = NZ * PLANE
    return pl.pallas_call(
        kernel,
        out_shape=jax.ShapeDtypeStruct((OWN, D), bf16),
        in_specs=[pl.BlockSpec(memory_space=pltpu.HBM)] * 3,
        out_specs=pl.BlockSpec(memory_space=pltpu.VMEM),
        scratch_shapes=[
            pltpu.VMEM((OWN, D), bf16),
            pltpu.VMEM((OWN, D // 32), jnp.int32),
            pltpu.VMEM((VDEV, D), bf16),
            pltpu.VMEM((D, VDEV), bf16),
            pltpu.VMEM((NZ, 2, NX, 2 * OWN, HALF), bf16),
            pltpu.VMEM((n, D), bf16),
            pltpu.VMEM((NCHUNK, CHUNK, VDEV), f32),
            pltpu.VMEM((n, VDEV), bf16),
            pltpu.VMEM((n, WIDE), f32),
            pltpu.VMEM((NZ, PAIR, WIDE), f32),
            pltpu.VMEM((NZ, NX, 2 * OWN, MSG), bf16),
            pltpu.VMEM((NZ, NX, 2 * OWN, MSG), bf16),
            pltpu.VMEM((NZ, OWN, WIDE), f32),
            pltpu.VMEM((NZ, 2 * OWN, MSG), bf16),
            pltpu.VMEM((NZ, 2 * OWN, MSG), bf16),
            dma((LOADS,)), dma((2,)),
            dma((NZ, NX)), dma((NZ, NX)),
            dma((NZ,)), dma((NZ,)),
            dma((NZ, 2)), dma((NZ, 2)),
            dma((NZ, NX)), dma((NZ, NX)),
            dma((NZ,)), dma((NZ,)),
        ],
        compiler_params=pltpu.CompilerParams(
            collective_id=0, has_side_effects=True, vmem_limit_bytes=56 * 2**20
        ),
    )(codes, exps, text_bank)


def solution(mesh):
    return jax.shard_map(
        local,
        mesh=mesh,
        in_specs=(P(("dp", "bank"), None), P(("dp", "bank"), None), P("bank", None)),
        out_specs=P(("dp", "bank"), None),
        check_vma=False,
    )
```

```python
import math

import jax
import jax.numpy as jnp
from jax import lax
from jax.experimental import pallas as pl
from jax.experimental.pallas import tpu as pltpu
from jax.sharding import PartitionSpec as P

MESH = pl.DeviceIdType.MESH
D = 1024
HALF = D // 2
VDEV = 4096
NZ, NX = 8, 4
OWN = 8
PAIR = NX * OWN
PLANE = 2 * PAIR
WIDE = D + 128
MSG = HALF + 128
SLOTS = (0, 1, 7, 4, 3, 5, 2, 6)
FIRST = ((0, 3), (3, 6), (6, 8))
SECOND = ((0, 3), (3, 6), (6, 8))
LOADS = 8
QTILE = 512
DIRECT_IN = (0, 1, 7)
DIRECT_OUT = (0, 1, 7)
BUNDLE_IN = (2, 6)
SENDS = (
    (0, 2), (0, 1), (0, 3), (4, 0), (3, 0), (5, 0), (1, 2), (1, 1), (1, 3), (1, 0), (7, 2), (7, 1), (7, 3), (7,
    0),
)
STEPS = (
    ("t", 0), ("t", 1), ("t", 2), ("t", 3), ("t", 4), ("t", 5), ("t", 6), ("t", 7), ("swap", 0), ("bundle", 2),
    ("bundle", 6), ("fwd", 3), ("fwd", 5), ("fwd", 4), ("swap", 1), ("swap", 7), ("pack", 0), ("pack", 1),
    ("pack", 2), ("q", 0), ("swap", 3), ("swap", 5), ("swap", 4), ("swap", 2), ("swap", 6), ("w", 0), ("va", 0),
    ("vb", 0), ("pack", 3), ("pack", 4), ("pack", 5), ("q", 1), ("pair", 0), ("pair", 1), ("pair", 2), ("w", 1),
    ("va", 1), ("vb", 1), ("pack", 6), ("pack", 7), ("q", 2), ("w", 2), ("va", 2), ("pair", 3), ("pair", 4),
    ("pair", 5), ("vb", 2), ("end", 0), ("end", 1), ("end", 7), ("pair", 6), ("pair", 7), ("x", 3), ("x", 4),
    ("x", 5), ("x", 6), ("x", 7), ("end", 3), ("end", 5), ("end", 4), ("end", 2), ("end", 6),
)
SCALE = 2.0 / math.log(2.0)


def merge(parts):
    top = parts[0][0]
    for m, _, _ in parts[1:]:
        top = jnp.maximum(top, m)
    total, rows = None, None
    for m, s, p in parts:
        f = jnp.exp2((m - top) * SCALE)
        total = s * f if total is None else total + s * f
        rows = p * f if rows is None else rows + p * f
    return top, total, rows


def pack_ms(m, s):
    lane = lax.broadcasted_iota(jnp.int32, (m.shape[0], 128), 1)
    return jnp.where(lane < 64, m, s)


def unpack(wide):
    return wide[:, D : D + 1], wide[:, D + 64 : D + 65], wide[:, :D]


def to_travel(rows):
    return jnp.concatenate([rows[:, :HALF], rows[:, HALF:]], axis=0)


def from_travel(block):
    return jnp.concatenate([block[:OWN], block[OWN:]], axis=1)


def to_message(m, s, rows):
    col = jnp.broadcast_to(jnp.concatenate([m, s], axis=0), (2 * OWN, 128))
    hi = col.astype(jnp.bfloat16).astype(jnp.float32)
    mid = (col - hi).astype(jnp.bfloat16).astype(jnp.float32)
    low = (col - hi) - mid
    lane = lax.broadcasted_iota(jnp.int32, col.shape, 1)
    tail = jnp.where(lane < 32, hi, jnp.where(lane < 64, mid, low))
    return jnp.concatenate([to_travel(rows), tail], axis=1).astype(jnp.bfloat16)


def from_message(block):
    wide = block.astype(jnp.float32)
    tail = wide[:, HALF:]
    col = (tail[:, 0:1] + tail[:, 32:33]) + tail[:, 64:65]
    return col[:OWN], col[OWN:], from_travel(wide[:, :HALF])


def kernel(
    codes_hbm, exps_hbm, text_hbm, out_ref,
    codes, exps, text, textt, gath, regs, logit, wgt, pbuf, cbuf, xsend, xb, qown, zsend, zb,
    load_sem, in_sem, gx_s, gx_r, gc_s, gc_r, rc_s, rc_r, rx_s, rx_r, rz_s, rz_r,
):
    me = lax.axis_index("bank")
    z, x, c = me // (2 * NX), (me // 2) % NX, me % 2

    def at(dz, dx, dc):
        return {"bank": ((z + dz) % NZ) * (2 * NX) + ((x + dx) % NX) * 2 + (c + dc) % 2}

    def remote(src, dst, s, r, dev):
        return pltpu.make_async_remote_copy(
            src_ref=src, dst_ref=dst, send_sem=s, recv_sem=r, device_id=dev, device_id_type=MESH
        )

    barrier = pltpu.get_barrier_semaphore()
    far = [(d, 0, 0) for d in (4, 3, 5, 2, 6)]
    near = [(d, i, 0) for d in sorted((set(DIRECT_IN) | set(DIRECT_OUT)) - {0}) for i in range(1, NX)]
    peers = far + near + [(1, 0, 0), (7, 0, 0), (0, 2, 0), (0, 1, 0), (0, 3, 0), (0, 0, 1)]
    for p in peers:
        pl.semaphore_signal(barrier, inc=1, device_id=at(*p), device_id_type=MESH)

    in_codes = pltpu.make_async_copy(codes_hbm, codes, in_sem.at[0])
    in_exps = pltpu.make_async_copy(exps_hbm, exps, in_sem.at[1])
    in_codes.start()
    in_exps.start()
    span = VDEV // LOADS
    loads = [
        pltpu.make_async_copy(
            text_hbm.at[pl.ds(k * span, span)], text.at[pl.ds(k * span, span)], load_sem.at[k]
        )
        for k in range(LOADS)
    ]
    for ld in loads:
        ld.start()

    feat = lax.broadcasted_iota(jnp.int32, (32, D), 1) // 32
    blk = lax.broadcasted_iota(jnp.int32, (32, D), 0)
    spread = jnp.where(feat == blk, 1.0, 0.0).astype(jnp.bfloat16)
    in_codes.wait()
    in_exps.wait()
    scale = jnp.exp2(exps[...].astype(jnp.float32)).astype(jnp.bfloat16)
    expanded = jnp.dot(scale, spread, preferred_element_type=jnp.float32)
    own = codes[...].astype(jnp.float32) * expanded
    gath[0, 0, 0] = to_travel(own).astype(jnp.bfloat16)
    pl.semaphore_wait(barrier, len(peers))

    started = []

    def go(copy):
        copy.start()
        started.append(copy)
        return copy

    gx, gc = {}, {}

    def send(e, i):
        d, j = (NZ - e) % NZ, (NX - i) % NX
        gx[d, j] = go(remote(gath.at[0, 0, 0], gath.at[d, 0, j], gx_s.at[d, j], gx_r.at[d, j], at(e, i, 0)))

    def forward(d):
        gx[d, 0].wait_recv()
        for i in (2, 1, 3):
            j = NX - i
            gx[d, j] = go(remote(gath.at[d, 0, 0], gath.at[d, 0, j], gx_s.at[d, j], gx_r.at[d, j], at(0, i, 0)))

    def bundle(e):
        d = (NZ - e) % NZ
        gx[d, 0] = go(remote(gath.at[0, 0], gath.at[d, 0], gx_s.at[d, 0], gx_r.at[d, 0], at(e, 0, 0)))

    def swap(d):
        if d in BUNDLE_IN:
            gx[d, 0].wait_recv()
        else:
            for j in range(NX):
                if j or (d and d in DIRECT_IN):
                    gx[d, j].wait_recv()
        gc[d] = go(remote(gath.at[d, 0], gath.at[d, 1], gc_s.at[d], gc_r.at[d], at(0, 0, 1)))

    def transpose(k):
        loads[k].wait()
        textt[:, k * span : (k + 1) * span] = text[k * span : (k + 1) * span, :].T

    def repack(slot):
        d = SLOTS[slot]
        gc[d].wait_recv()
        for cr in range(2):
            for i in range(0, NX, 2):
                a = from_travel(gath[d, cr, i].astype(jnp.float32))
                b = from_travel(gath[d, cr, i + 1].astype(jnp.float32))
                r0 = slot * PLANE + cr * PAIR + i * OWN
                regs[r0 : r0 + 2 * OWN, :] = jnp.concatenate([a, b], axis=0).astype(jnp.bfloat16)

    top = {}

    def logits(g):
        lo, hi = FIRST[g][0] * PLANE, FIRST[g][1] * PLANE
        peak = jnp.full((hi - lo, 128), -jnp.inf, jnp.float32)
        for t in range(VDEV // QTILE):
            dots = jnp.dot(
                regs[lo:hi, :], textt[:, t * QTILE : (t + 1) * QTILE], preferred_element_type=jnp.float32
            )
            logit[lo:hi, t * QTILE : (t + 1) * QTILE] = dots
            for q in range(QTILE // 128):
                peak = jnp.maximum(peak, dots[:, q * 128 : (q + 1) * 128])
        top[g] = jnp.max(peak, axis=1, keepdims=True)

    def weights(g):
        lo, hi = FIRST[g][0] * PLANE, FIRST[g][1] * PLANE
        total = jnp.zeros((hi - lo, 128), jnp.float32)
        for k in range(VDEV // 128):
            e = jnp.exp2((logit[lo:hi, k * 128 : (k + 1) * 128] - top[g]) * SCALE)
            total = total + e
            wgt[lo:hi, k * 128 : (k + 1) * 128] = e.astype(jnp.bfloat16)
        pbuf[lo:hi, D:] = pack_ms(top[g], jnp.sum(total, axis=1, keepdims=True))

    rc, rx, rz = {}, {}, {}

    def values(h, k):
        lo, hi = SECOND[h][0] * PLANE, SECOND[h][1] * PLANE
        pbuf[lo:hi, k * HALF : (k + 1) * HALF] = jnp.dot(
            wgt[lo:hi, :], text[:, k * HALF : (k + 1) * HALF], preferred_element_type=jnp.float32
        )
        cols = pl.ds(0, HALF) if k == 0 else pl.ds(HALF, WIDE - HALF)
        for slot in range(*SECOND[h]):
            rc[slot, k] = go(remote(
                pbuf.at[pl.ds(slot * PLANE + PAIR, PAIR), cols], cbuf.at[slot, :, cols],
                rc_s.at[slot, k], rc_r.at[slot, k], at(0, 0, 1),
            ))

    def pair_sum(slot):
        d = SLOTS[slot]
        rc[slot, 0].wait_recv()
        rc[slot, 1].wait_recv()
        lo = slot * PLANE
        m, s, p = merge([unpack(pbuf[lo : lo + PAIR, :]), unpack(cbuf[slot])])
        straight = d in DIRECT_OUT
        e = (NZ - d) % NZ if straight else d
        for i in (2, 1, 3, 0):
            j = (NX - i) % NX
            lo, hi = i * OWN, (i + 1) * OWN
            if i == 0 and not (straight and d):
                qown[slot, :, :D] = p[lo:hi]
                qown[slot, :, D:] = pack_ms(m[lo:hi], s[lo:hi])
                continue
            xsend[d, i] = to_message(m[lo:hi], s[lo:hi], p[lo:hi])
            rx[e, j] = go(remote(
                xsend.at[d, i], xb.at[e, j], rx_s.at[d, i], rx_r.at[e, j], at(d if straight else 0, i, 0)
            ))

    def plane(e, first):
        parts = list(first)
        for j in range(NX):
            if j or not first:
                rx[e, j].wait_recv()
                parts.append(from_message(xb[e, j]))
        return parts

    def x_sum(slot):
        d = SLOTS[slot]
        m, s, p = merge(plane(d, [unpack(qown[slot])]))
        zsend[d] = to_message(m, s, p)
        e = (NZ - d) % NZ
        rz[e] = go(remote(zsend.at[d], zb.at[e], rz_s.at[e], rz_r.at[e], at(d, 0, 0)))

    result = []

    def collect(e):
        if e == 0:
            parts = plane(0, [unpack(qown[0])])
        elif e in DIRECT_OUT:
            parts = plane(e, [])
        else:
            rz[e].wait_recv()
            parts = [from_message(zb[e])]
        result[:] = [merge(result + parts)]

    run = {
        "t": transpose, "fwd": forward, "bundle": bundle, "swap": swap, "pack": repack, "q": logits, "w": weights,
        "va": lambda h: values(h, 0), "vb": lambda h: values(h, 1), "pair": pair_sum, "x": x_sum, "end": collect,
    }
    for e, i in SENDS:
        send(e, i)
    for name, k in STEPS:
        run[name](k)
    m, s, p = result[0]
    out_ref[...] = (p / s).astype(jnp.bfloat16)
    for cp in started:
        cp.wait_send()


def local(codes, exps, text_bank):
    dma = pltpu.SemaphoreType.DMA
    f32, bf16 = jnp.float32, jnp.bfloat16
    n = NZ * PLANE
    return pl.pallas_call(
        kernel,
        out_shape=jax.ShapeDtypeStruct((OWN, D), bf16),
        in_specs=[pl.BlockSpec(memory_space=pltpu.HBM)] * 3,
        out_specs=pl.BlockSpec(memory_space=pltpu.VMEM),
        scratch_shapes=[
            pltpu.VMEM((OWN, D), bf16),
            pltpu.VMEM((OWN, D // 32), jnp.int32),
            pltpu.VMEM((VDEV, D), bf16),
            pltpu.VMEM((D, VDEV), bf16),
            pltpu.VMEM((NZ, 2, NX, 2 * OWN, HALF), bf16),
            pltpu.VMEM((n, D), bf16),
            pltpu.VMEM((n, VDEV), f32),
            pltpu.VMEM((n, VDEV), bf16),
            pltpu.VMEM((n, WIDE), f32),
            pltpu.VMEM((NZ, PAIR, WIDE), f32),
            pltpu.VMEM((NZ, NX, 2 * OWN, MSG), bf16),
            pltpu.VMEM((NZ, NX, 2 * OWN, MSG), bf16),
            pltpu.VMEM((NZ, OWN, WIDE), f32),
            pltpu.VMEM((NZ, 2 * OWN, MSG), bf16),
            pltpu.VMEM((NZ, 2 * OWN, MSG), bf16),
            dma((LOADS,)), dma((2,)),
            dma((NZ, NX)), dma((NZ, NX)),
            dma((NZ,)), dma((NZ,)),
            dma((NZ, 2)), dma((NZ, 2)),
            dma((NZ, NX)), dma((NZ, NX)),
            dma((NZ,)), dma((NZ,)),
        ],
        compiler_params=pltpu.CompilerParams(
            collective_id=0, has_side_effects=True, vmem_limit_bytes=56 * 2**20
        ),
    )(codes, exps, text_bank)


def solution(mesh):
    return jax.shard_map(
        local,
        mesh=mesh,
        in_specs=(P(("dp", "bank"), None), P(("dp", "bank"), None), P("bank", None)),
        out_specs=P(("dp", "bank"), None),
        check_vma=False,
    )
```

```python
import math

import jax
import jax.numpy as jnp
from jax import lax
from jax.experimental import pallas as pl
from jax.experimental.pallas import tpu as pltpu
from jax.sharding import PartitionSpec as P

MESH = pl.DeviceIdType.MESH
D = 1024
HALF = D // 2
VDEV = 4096
NZ, NX = 8, 4
OWN = 8
PAIR = NX * OWN
PLANE = 2 * PAIR
WIDE = D + 128
MSG = HALF + 128
SLOTS = (0, 1, 7, 4, 3, 5, 2, 6)
FIRST = ((0, 3), (3, 6), (6, 8))
SECOND = ((0, 3), (3, 6), (6, 8))
LOADS = 8
QTILE = 512
DIRECT_IN = (0, 1, 7)
DIRECT_OUT = (0, 1, 7)
BUNDLE_IN = (2, 6)
SENDS = (
    (0, 2), (0, 1), (0, 3), (4, 0), (3, 0), (5, 0), (1, 2), (1, 1), (1, 3), (1, 0), (7, 2), (7, 1), (7, 3), (7,
    0),
)
STEPS = (
    ("t", 0), ("t", 1), ("t", 2), ("swap", 0), ("bundle", 2), ("bundle", 6), ("fwd", 3), ("fwd", 5), ("t", 3),
    ("fwd", 4), ("swap", 1), ("swap", 7), ("t", 4), ("t", 5), ("t", 6), ("t", 7), ("pack", 0), ("pack", 1),
    ("pack", 2), ("q", 0), ("swap", 3), ("swap", 5), ("swap", 4), ("swap", 2), ("swap", 6), ("w", 0), ("va", 0),
    ("vb", 0), ("pack", 3), ("pack", 4), ("pack", 5), ("q", 1), ("pair", 0), ("pair", 1), ("pair", 2), ("w", 1),
    ("va", 1), ("vb", 1), ("pack", 6), ("pack", 7), ("q", 2), ("w", 2), ("va", 2), ("pair", 3), ("pair", 4),
    ("pair", 5), ("vb", 2), ("end", 0), ("end", 1), ("end", 7), ("pair", 6), ("pair", 7), ("x", 3), ("x", 4),
    ("x", 5), ("x", 6), ("x", 7), ("end", 3), ("end", 5), ("end", 4), ("end", 2), ("end", 6),
)
SCALE = 2.0 / math.log(2.0)


def merge(parts):
    top = parts[0][0]
    for m, _, _ in parts[1:]:
        top = jnp.maximum(top, m)
    total, rows = None, None
    for m, s, p in parts:
        f = jnp.exp2((m - top) * SCALE)
        total = s * f if total is None else total + s * f
        rows = p * f if rows is None else rows + p * f
    return top, total, rows


def pack_ms(m, s):
    lane = lax.broadcasted_iota(jnp.int32, (m.shape[0], 128), 1)
    return jnp.where(lane < 64, m, s)


def unpack(wide):
    return wide[:, D : D + 1], wide[:, D + 64 : D + 65], wide[:, :D]


def to_travel(rows):
    return jnp.concatenate([rows[:, :HALF], rows[:, HALF:]], axis=0)


def from_travel(block):
    return jnp.concatenate([block[:OWN], block[OWN:]], axis=1)


def to_message(m, s, rows):
    col = jnp.broadcast_to(jnp.concatenate([m, s], axis=0), (2 * OWN, 128))
    hi = col.astype(jnp.bfloat16).astype(jnp.float32)
    mid = (col - hi).astype(jnp.bfloat16).astype(jnp.float32)
    low = (col - hi) - mid
    lane = lax.broadcasted_iota(jnp.int32, col.shape, 1)
    tail = jnp.where(lane < 32, hi, jnp.where(lane < 64, mid, low))
    return jnp.concatenate([to_travel(rows), tail], axis=1).astype(jnp.bfloat16)


def from_message(block):
    wide = block.astype(jnp.float32)
    tail = wide[:, HALF:]
    col = (tail[:, 0:1] + tail[:, 32:33]) + tail[:, 64:65]
    return col[:OWN], col[OWN:], from_travel(wide[:, :HALF])


def kernel(
    codes_hbm, exps_hbm, text_hbm, out_ref,
    codes, exps, text, textt, gath, regs, logit, wgt, pbuf, cbuf, xsend, xb, qown, zsend, zb,
    load_sem, in_sem, gx_s, gx_r, gc_s, gc_r, rc_s, rc_r, rx_s, rx_r, rz_s, rz_r,
):
    me = lax.axis_index("bank")
    z, x, c = me // (2 * NX), (me // 2) % NX, me % 2

    def at(dz, dx, dc):
        return {"bank": ((z + dz) % NZ) * (2 * NX) + ((x + dx) % NX) * 2 + (c + dc) % 2}

    def remote(src, dst, s, r, dev):
        return pltpu.make_async_remote_copy(
            src_ref=src, dst_ref=dst, send_sem=s, recv_sem=r, device_id=dev, device_id_type=MESH
        )

    barrier = pltpu.get_barrier_semaphore()
    far = [(d, 0, 0) for d in (4, 3, 5, 2, 6)]
    near = [(d, i, 0) for d in sorted((set(DIRECT_IN) | set(DIRECT_OUT)) - {0}) for i in range(1, NX)]
    peers = far + near + [(1, 0, 0), (7, 0, 0), (0, 2, 0), (0, 1, 0), (0, 3, 0), (0, 0, 1)]
    for p in peers:
        pl.semaphore_signal(barrier, inc=1, device_id=at(*p), device_id_type=MESH)

    in_codes = pltpu.make_async_copy(codes_hbm, codes, in_sem.at[0])
    in_exps = pltpu.make_async_copy(exps_hbm, exps, in_sem.at[1])
    in_codes.start()
    in_exps.start()
    span = VDEV // LOADS
    loads = [
        pltpu.make_async_copy(
            text_hbm.at[pl.ds(k * span, span)], text.at[pl.ds(k * span, span)], load_sem.at[k]
        )
        for k in range(LOADS)
    ]
    for ld in loads:
        ld.start()

    feat = lax.broadcasted_iota(jnp.int32, (32, D), 1) // 32
    blk = lax.broadcasted_iota(jnp.int32, (32, D), 0)
    spread = jnp.where(feat == blk, 1.0, 0.0).astype(jnp.bfloat16)
    in_codes.wait()
    in_exps.wait()
    scale = jnp.exp2(exps[...].astype(jnp.float32)).astype(jnp.bfloat16)
    expanded = jnp.dot(scale, spread, preferred_element_type=jnp.float32)
    own = codes[...].astype(jnp.float32) * expanded
    gath[0, 0, 0] = to_travel(own).astype(jnp.bfloat16)
    pl.semaphore_wait(barrier, len(peers))

    started = []

    def go(copy):
        copy.start()
        started.append(copy)
        return copy

    gx, gc = {}, {}

    def send(e, i):
        d, j = (NZ - e) % NZ, (NX - i) % NX
        gx[d, j] = go(remote(gath.at[0, 0, 0], gath.at[d, 0, j], gx_s.at[d, j], gx_r.at[d, j], at(e, i, 0)))

    def forward(d):
        gx[d, 0].wait_recv()
        for i in (2, 1, 3):
            j = NX - i
            gx[d, j] = go(remote(gath.at[d, 0, 0], gath.at[d, 0, j], gx_s.at[d, j], gx_r.at[d, j], at(0, i, 0)))

    def bundle(e):
        d = (NZ - e) % NZ
        gx[d, 0] = go(remote(gath.at[0, 0], gath.at[d, 0], gx_s.at[d, 0], gx_r.at[d, 0], at(e, 0, 0)))

    def swap(d):
        if d in BUNDLE_IN:
            gx[d, 0].wait_recv()
        else:
            for j in range(NX):
                if j or (d and d in DIRECT_IN):
                    gx[d, j].wait_recv()
        gc[d] = go(remote(gath.at[d, 0], gath.at[d, 1], gc_s.at[d], gc_r.at[d], at(0, 0, 1)))

    def transpose(k):
        loads[k].wait()
        textt[:, k * span : (k + 1) * span] = text[k * span : (k + 1) * span, :].T

    def repack(slot):
        d = SLOTS[slot]
        gc[d].wait_recv()
        for cr in range(2):
            for i in range(0, NX, 2):
                a = from_travel(gath[d, cr, i].astype(jnp.float32))
                b = from_travel(gath[d, cr, i + 1].astype(jnp.float32))
                r0 = slot * PLANE + cr * PAIR + i * OWN
                regs[r0 : r0 + 2 * OWN, :] = jnp.concatenate([a, b], axis=0).astype(jnp.bfloat16)

    top = {}

    def logits(g):
        lo, hi = FIRST[g][0] * PLANE, FIRST[g][1] * PLANE
        peak = jnp.full((hi - lo, 128), -jnp.inf, jnp.float32)
        for t in range(VDEV // QTILE):
            dots = jnp.dot(
                regs[lo:hi, :], textt[:, t * QTILE : (t + 1) * QTILE], preferred_element_type=jnp.float32
            )
            logit[lo:hi, t * QTILE : (t + 1) * QTILE] = dots
            for q in range(QTILE // 128):
                peak = jnp.maximum(peak, dots[:, q * 128 : (q + 1) * 128])
        top[g] = jnp.max(peak, axis=1, keepdims=True)

    def weights(g):
        lo, hi = FIRST[g][0] * PLANE, FIRST[g][1] * PLANE
        total = jnp.zeros((hi - lo, 128), jnp.float32)
        for k in range(VDEV // 128):
            e = jnp.exp2((logit[lo:hi, k * 128 : (k + 1) * 128] - top[g]) * SCALE)
            total = total + e
            wgt[lo:hi, k * 128 : (k + 1) * 128] = e.astype(jnp.bfloat16)
        pbuf[lo:hi, D:] = pack_ms(top[g], jnp.sum(total, axis=1, keepdims=True))

    rc, rx, rz = {}, {}, {}

    def values(h, k):
        lo, hi = SECOND[h][0] * PLANE, SECOND[h][1] * PLANE
        pbuf[lo:hi, k * HALF : (k + 1) * HALF] = jnp.dot(
            wgt[lo:hi, :], text[:, k * HALF : (k + 1) * HALF], preferred_element_type=jnp.float32
        )
        cols = pl.ds(0, HALF) if k == 0 else pl.ds(HALF, WIDE - HALF)
        for slot in range(*SECOND[h]):
            rc[slot, k] = go(remote(
                pbuf.at[pl.ds(slot * PLANE + PAIR, PAIR), cols], cbuf.at[slot, :, cols],
                rc_s.at[slot, k], rc_r.at[slot, k], at(0, 0, 1),
            ))

    def pair_sum(slot):
        d = SLOTS[slot]
        rc[slot, 0].wait_recv()
        rc[slot, 1].wait_recv()
        lo = slot * PLANE
        m, s, p = merge([unpack(pbuf[lo : lo + PAIR, :]), unpack(cbuf[slot])])
        straight = d in DIRECT_OUT
        e = (NZ - d) % NZ if straight else d
        for i in (2, 1, 3, 0):
            j = (NX - i) % NX
            lo, hi = i * OWN, (i + 1) * OWN
            if i == 0 and not (straight and d):
                qown[slot, :, :D] = p[lo:hi]
                qown[slot, :, D:] = pack_ms(m[lo:hi], s[lo:hi])
                continue
            xsend[d, i] = to_message(m[lo:hi], s[lo:hi], p[lo:hi])
            rx[e, j] = go(remote(
                xsend.at[d, i], xb.at[e, j], rx_s.at[d, i], rx_r.at[e, j], at(d if straight else 0, i, 0)
            ))

    def plane(e, first):
        parts = list(first)
        for j in range(NX):
            if j or not first:
                rx[e, j].wait_recv()
                parts.append(from_message(xb[e, j]))
        return parts

    def x_sum(slot):
        d = SLOTS[slot]
        m, s, p = merge(plane(d, [unpack(qown[slot])]))
        zsend[d] = to_message(m, s, p)
        e = (NZ - d) % NZ
        rz[e] = go(remote(zsend.at[d], zb.at[e], rz_s.at[e], rz_r.at[e], at(d, 0, 0)))

    result = []

    def collect(e):
        if e == 0:
            parts = plane(0, [unpack(qown[0])])
        elif e in DIRECT_OUT:
            parts = plane(e, [])
        else:
            rz[e].wait_recv()
            parts = [from_message(zb[e])]
        result[:] = [merge(result + parts)]

    run = {
        "t": transpose, "fwd": forward, "bundle": bundle, "swap": swap, "pack": repack, "q": logits, "w": weights,
        "va": lambda h: values(h, 0), "vb": lambda h: values(h, 1), "pair": pair_sum, "x": x_sum, "end": collect,
    }
    for e, i in SENDS:
        send(e, i)
    for name, k in STEPS:
        run[name](k)
    m, s, p = result[0]
    out_ref[...] = (p / s).astype(jnp.bfloat16)
    for cp in started:
        cp.wait_send()


def local(codes, exps, text_bank):
    dma = pltpu.SemaphoreType.DMA
    f32, bf16 = jnp.float32, jnp.bfloat16
    n = NZ * PLANE
    return pl.pallas_call(
        kernel,
        out_shape=jax.ShapeDtypeStruct((OWN, D), bf16),
        in_specs=[pl.BlockSpec(memory_space=pltpu.HBM)] * 3,
        out_specs=pl.BlockSpec(memory_space=pltpu.VMEM),
        scratch_shapes=[
            pltpu.VMEM((OWN, D), bf16),
            pltpu.VMEM((OWN, D // 32), jnp.int32),
            pltpu.VMEM((VDEV, D), bf16),
            pltpu.VMEM((D, VDEV), bf16),
            pltpu.VMEM((NZ, 2, NX, 2 * OWN, HALF), bf16),
            pltpu.VMEM((n, D), bf16),
            pltpu.VMEM((n, VDEV), f32),
            pltpu.VMEM((n, VDEV), bf16),
            pltpu.VMEM((n, WIDE), f32),
            pltpu.VMEM((NZ, PAIR, WIDE), f32),
            pltpu.VMEM((NZ, NX, 2 * OWN, MSG), bf16),
            pltpu.VMEM((NZ, NX, 2 * OWN, MSG), bf16),
            pltpu.VMEM((NZ, OWN, WIDE), f32),
            pltpu.VMEM((NZ, 2 * OWN, MSG), bf16),
            pltpu.VMEM((NZ, 2 * OWN, MSG), bf16),
            dma((LOADS,)), dma((2,)),
            dma((NZ, NX)), dma((NZ, NX)),
            dma((NZ,)), dma((NZ,)),
            dma((NZ, 2)), dma((NZ, 2)),
            dma((NZ, NX)), dma((NZ, NX)),
            dma((NZ,)), dma((NZ,)),
        ],
        compiler_params=pltpu.CompilerParams(
            collective_id=0, has_side_effects=True, vmem_limit_bytes=56 * 2**20
        ),
    )(codes, exps, text_bank)


def solution(mesh):
    return jax.shard_map(
        local,
        mesh=mesh,
        in_specs=(P(("dp", "bank"), None), P(("dp", "bank"), None), P("bank", None)),
        out_specs=P(("dp", "bank"), None),
        check_vma=False,
    )
```

```python
import math

import jax
import jax.numpy as jnp
from jax import lax
from jax.experimental import pallas as pl
from jax.experimental.pallas import tpu as pltpu
from jax.sharding import PartitionSpec as P

MESH = pl.DeviceIdType.MESH
D = 1024
HALF = D // 2
VDEV = 4096
NZ, NX = 8, 4
OWN = 8
PAIR = NX * OWN
PLANE = 2 * PAIR
WIDE = D + 128
MSG = HALF + 128
SLOTS = (0, 1, 7, 4, 3, 5, 2, 6)
FIRST = ((0, 3), (3, 6), (6, 8))
SECOND = ((0, 3), (3, 6), (6, 8))
LOADS = 8
QTILE = 512
DIRECT_IN = (0, 1, 7)
DIRECT_OUT = (0, 1, 7)
BUNDLE_IN = (2, 6)
SENDS = (
    (0, 2), (0, 1), (0, 3), (4, 0), (3, 0), (5, 0), (1, 2), (1, 1), (1, 3), (1, 0), (7, 2), (7, 1), (7, 3), (7,
    0),
)
STEPS = (
    ("t", 0), ("t", 1), ("t", 2), ("swap", 0), ("bundle", 2), ("bundle", 6), ("fwd", 3), ("fwd", 5), ("t", 3),
    ("fwd", 4), ("swap", 1), ("swap", 7), ("t", 4), ("t", 5), ("t", 6), ("t", 7), ("pack", 0), ("pack", 1),
    ("pack", 2), ("q", 0), ("swap", 3), ("swap", 5), ("swap", 4), ("swap", 2), ("swap", 6), ("w", 0), ("va", 0),
    ("vb", 0), ("pack", 3), ("pack", 4), ("pack", 5), ("q", 1), ("pair", 0), ("pair", 1), ("pair", 2), ("w", 1),
    ("va", 1), ("vb", 1), ("pack", 6), ("pack", 7), ("q", 2), ("w", 2), ("va", 2), ("pair", 3), ("pair", 4),
    ("pair", 5), ("vb", 2), ("end", 0), ("end", 1), ("end", 7), ("sent", 11), ("pair", 6), ("pair", 7), ("x", 3), ("x", 4),
    ("x", 5), ("x", 6), ("x", 7), ("sent", 5), ("end", 3), ("end", 5), ("end", 4), ("end", 2), ("end", 6),
)
SCALE = 2.0 / math.log(2.0)


def merge(parts):
    top = parts[0][0]
    for m, _, _ in parts[1:]:
        top = jnp.maximum(top, m)
    total, rows = None, None
    for m, s, p in parts:
        f = jnp.exp2((m - top) * SCALE)
        total = s * f if total is None else total + s * f
        rows = p * f if rows is None else rows + p * f
    return top, total, rows


def pack_ms(m, s):
    lane = lax.broadcasted_iota(jnp.int32, (m.shape[0], 128), 1)
    return jnp.where(lane < 64, m, s)


def unpack(wide):
    return wide[:, D : D + 1], wide[:, D + 64 : D + 65], wide[:, :D]


def to_travel(rows):
    return jnp.concatenate([rows[:, :HALF], rows[:, HALF:]], axis=0)


def from_travel(block):
    return jnp.concatenate([block[:OWN], block[OWN:]], axis=1)


def to_message(m, s, rows):
    col = jnp.broadcast_to(jnp.concatenate([m, s], axis=0), (2 * OWN, 128))
    hi = col.astype(jnp.bfloat16).astype(jnp.float32)
    mid = (col - hi).astype(jnp.bfloat16).astype(jnp.float32)
    low = (col - hi) - mid
    lane = lax.broadcasted_iota(jnp.int32, col.shape, 1)
    tail = jnp.where(lane < 32, hi, jnp.where(lane < 64, mid, low))
    return jnp.concatenate([to_travel(rows), tail], axis=1).astype(jnp.bfloat16)


def from_message(block):
    wide = block.astype(jnp.float32)
    tail = wide[:, HALF:]
    col = (tail[:, 0:1] + tail[:, 32:33]) + tail[:, 64:65]
    return col[:OWN], col[OWN:], from_travel(wide[:, :HALF])


def kernel(
    codes_hbm, exps_hbm, text_hbm, out_ref,
    codes, exps, text, textt, gath, regs, logit, wgt, pbuf, cbuf, xsend, xb, qown, zsend, zb,
    load_sem, in_sem, gx_s, gx_r, gc_s, gc_r, rc_s, rc_r, rx_s, rx_r, rz_s, rz_r,
):
    me = lax.axis_index("bank")
    z, x, c = me // (2 * NX), (me // 2) % NX, me % 2

    def at(dz, dx, dc):
        return {"bank": ((z + dz) % NZ) * (2 * NX) + ((x + dx) % NX) * 2 + (c + dc) % 2}

    def remote(src, dst, s, r, dev):
        return pltpu.make_async_remote_copy(
            src_ref=src, dst_ref=dst, send_sem=s, recv_sem=r, device_id=dev, device_id_type=MESH
        )

    barrier = pltpu.get_barrier_semaphore()
    far = [(d, 0, 0) for d in (4, 3, 5, 2, 6)]
    near = [(d, i, 0) for d in sorted((set(DIRECT_IN) | set(DIRECT_OUT)) - {0}) for i in range(1, NX)]
    peers = far + near + [(1, 0, 0), (7, 0, 0), (0, 2, 0), (0, 1, 0), (0, 3, 0), (0, 0, 1)]
    for p in peers:
        pl.semaphore_signal(barrier, inc=1, device_id=at(*p), device_id_type=MESH)

    in_codes = pltpu.make_async_copy(codes_hbm, codes, in_sem.at[0])
    in_exps = pltpu.make_async_copy(exps_hbm, exps, in_sem.at[1])
    in_codes.start()
    in_exps.start()
    span = VDEV // LOADS
    loads = [
        pltpu.make_async_copy(
            text_hbm.at[pl.ds(k * span, span)], text.at[pl.ds(k * span, span)], load_sem.at[k]
        )
        for k in range(LOADS)
    ]
    for ld in loads:
        ld.start()

    feat = lax.broadcasted_iota(jnp.int32, (32, D), 1) // 32
    blk = lax.broadcasted_iota(jnp.int32, (32, D), 0)
    spread = jnp.where(feat == blk, 1.0, 0.0).astype(jnp.bfloat16)
    in_codes.wait()
    in_exps.wait()
    scale = jnp.exp2(exps[...].astype(jnp.float32)).astype(jnp.bfloat16)
    expanded = jnp.dot(scale, spread, preferred_element_type=jnp.float32)
    own = codes[...].astype(jnp.float32) * expanded
    gath[0, 0, 0] = to_travel(own).astype(jnp.bfloat16)
    pl.semaphore_wait(barrier, len(peers))

    started = []

    def go(copy):
        copy.start()
        started.append(copy)
        return copy

    gx, gc = {}, {}

    def send(e, i):
        d, j = (NZ - e) % NZ, (NX - i) % NX
        gx[d, j] = go(remote(gath.at[0, 0, 0], gath.at[d, 0, j], gx_s.at[d, j], gx_r.at[d, j], at(e, i, 0)))

    def forward(d):
        gx[d, 0].wait_recv()
        for i in (2, 1, 3):
            j = NX - i
            gx[d, j] = go(remote(gath.at[d, 0, 0], gath.at[d, 0, j], gx_s.at[d, j], gx_r.at[d, j], at(0, i, 0)))

    def bundle(e):
        d = (NZ - e) % NZ
        gx[d, 0] = go(remote(gath.at[0, 0], gath.at[d, 0], gx_s.at[d, 0], gx_r.at[d, 0], at(e, 0, 0)))

    def swap(d):
        if d in BUNDLE_IN:
            gx[d, 0].wait_recv()
        else:
            for j in range(NX):
                if j or (d and d in DIRECT_IN):
                    gx[d, j].wait_recv()
        gc[d] = go(remote(gath.at[d, 0], gath.at[d, 1], gc_s.at[d], gc_r.at[d], at(0, 0, 1)))

    def transpose(k):
        loads[k].wait()
        textt[:, k * span : (k + 1) * span] = text[k * span : (k + 1) * span, :].T

    def repack(slot):
        d = SLOTS[slot]
        gc[d].wait_recv()
        for cr in range(2):
            for i in range(0, NX, 2):
                a = from_travel(gath[d, cr, i].astype(jnp.float32))
                b = from_travel(gath[d, cr, i + 1].astype(jnp.float32))
                r0 = slot * PLANE + cr * PAIR + i * OWN
                regs[r0 : r0 + 2 * OWN, :] = jnp.concatenate([a, b], axis=0).astype(jnp.bfloat16)

    top = {}

    def logits(g):
        lo, hi = FIRST[g][0] * PLANE, FIRST[g][1] * PLANE
        peak = jnp.full((hi - lo, 128), -jnp.inf, jnp.float32)
        for t in range(VDEV // QTILE):
            dots = jnp.dot(
                regs[lo:hi, :], textt[:, t * QTILE : (t + 1) * QTILE], preferred_element_type=jnp.float32
            )
            logit[lo:hi, t * QTILE : (t + 1) * QTILE] = dots
            for q in range(QTILE // 128):
                peak = jnp.maximum(peak, dots[:, q * 128 : (q + 1) * 128])
        top[g] = jnp.max(peak, axis=1, keepdims=True)

    def weights(g):
        lo, hi = FIRST[g][0] * PLANE, FIRST[g][1] * PLANE
        total = jnp.zeros((hi - lo, 128), jnp.float32)
        for k in range(VDEV // 128):
            e = jnp.exp2((logit[lo:hi, k * 128 : (k + 1) * 128] - top[g]) * SCALE)
            total = total + e
            wgt[lo:hi, k * 128 : (k + 1) * 128] = e.astype(jnp.bfloat16)
        pbuf[lo:hi, D:] = pack_ms(top[g], jnp.sum(total, axis=1, keepdims=True))

    rc, rx, rz = {}, {}, {}

    def values(h, k):
        lo, hi = SECOND[h][0] * PLANE, SECOND[h][1] * PLANE
        pbuf[lo:hi, k * HALF : (k + 1) * HALF] = jnp.dot(
            wgt[lo:hi, :], text[:, k * HALF : (k + 1) * HALF], preferred_element_type=jnp.float32
        )
        cols = pl.ds(0, HALF) if k == 0 else pl.ds(HALF, WIDE - HALF)
        for slot in range(*SECOND[h]):
            rc[slot, k] = go(remote(
                pbuf.at[pl.ds(slot * PLANE + PAIR, PAIR), cols], cbuf.at[slot, :, cols],
                rc_s.at[slot, k], rc_r.at[slot, k], at(0, 0, 1),
            ))

    def pair_sum(slot):
        d = SLOTS[slot]
        rc[slot, 0].wait_recv()
        rc[slot, 1].wait_recv()
        lo = slot * PLANE
        m, s, p = merge([unpack(pbuf[lo : lo + PAIR, :]), unpack(cbuf[slot])])
        straight = d in DIRECT_OUT
        e = (NZ - d) % NZ if straight else d
        for i in (2, 1, 3, 0):
            j = (NX - i) % NX
            lo, hi = i * OWN, (i + 1) * OWN
            if i == 0 and not (straight and d):
                qown[slot, :, :D] = p[lo:hi]
                qown[slot, :, D:] = pack_ms(m[lo:hi], s[lo:hi])
                continue
            xsend[d, i] = to_message(m[lo:hi], s[lo:hi], p[lo:hi])
            rx[e, j] = go(remote(
                xsend.at[d, i], xb.at[e, j], rx_s.at[d, i], rx_r.at[e, j], at(d if straight else 0, i, 0)
            ))

    def plane(e, first):
        parts = list(first)
        for j in range(NX):
            if j or not first:
                rx[e, j].wait_recv()
                parts.append(from_message(xb[e, j]))
        return parts

    def x_sum(slot):
        d = SLOTS[slot]
        m, s, p = merge(plane(d, [unpack(qown[slot])]))
        zsend[d] = to_message(m, s, p)
        e = (NZ - d) % NZ
        rz[e] = go(remote(zsend.at[d], zb.at[e], rz_s.at[e], rz_r.at[e], at(d, 0, 0)))

    result = []

    def collect(e):
        if e == 0:
            parts = plane(0, [unpack(qown[0])])
        elif e in DIRECT_OUT:
            parts = plane(e, [])
        else:
            rz[e].wait_recv()
            parts = [from_message(zb[e])]
        result[:] = [merge(result + parts)]

    def drain(keep):
        for copy in started[: len(started) - keep]:
            copy.wait_send()
        del started[: len(started) - keep]

    run = {
        "sent": drain, "t": transpose, "fwd": forward, "bundle": bundle, "swap": swap, "pack": repack, "q": logits, "w": weights,
        "va": lambda h: values(h, 0), "vb": lambda h: values(h, 1), "pair": pair_sum, "x": x_sum, "end": collect,
    }
    for e, i in SENDS:
        send(e, i)
    for name, k in STEPS:
        run[name](k)
    m, s, p = result[0]
    out_ref[...] = (p / s).astype(jnp.bfloat16)
    for cp in started:
        cp.wait_send()


def local(codes, exps, text_bank):
    dma = pltpu.SemaphoreType.DMA
    f32, bf16 = jnp.float32, jnp.bfloat16
    n = NZ * PLANE
    return pl.pallas_call(
        kernel,
        out_shape=jax.ShapeDtypeStruct((OWN, D), bf16),
        in_specs=[pl.BlockSpec(memory_space=pltpu.HBM)] * 3,
        out_specs=pl.BlockSpec(memory_space=pltpu.VMEM),
        scratch_shapes=[
            pltpu.VMEM((OWN, D), bf16),
            pltpu.VMEM((OWN, D // 32), jnp.int32),
            pltpu.VMEM((VDEV, D), bf16),
            pltpu.VMEM((D, VDEV), bf16),
            pltpu.VMEM((NZ, 2, NX, 2 * OWN, HALF), bf16),
            pltpu.VMEM((n, D), bf16),
            pltpu.VMEM((n, VDEV), f32),
            pltpu.VMEM((n, VDEV), bf16),
            pltpu.VMEM((n, WIDE), f32),
            pltpu.VMEM((NZ, PAIR, WIDE), f32),
            pltpu.VMEM((NZ, NX, 2 * OWN, MSG), bf16),
            pltpu.VMEM((NZ, NX, 2 * OWN, MSG), bf16),
            pltpu.VMEM((NZ, OWN, WIDE), f32),
            pltpu.VMEM((NZ, 2 * OWN, MSG), bf16),
            pltpu.VMEM((NZ, 2 * OWN, MSG), bf16),
            dma((LOADS,)), dma((2,)),
            dma((NZ, NX)), dma((NZ, NX)),
            dma((NZ,)), dma((NZ,)),
            dma((NZ, 2)), dma((NZ, 2)),
            dma((NZ, NX)), dma((NZ, NX)),
            dma((NZ,)), dma((NZ,)),
        ],
        compiler_params=pltpu.CompilerParams(
            collective_id=0, has_side_effects=True, vmem_limit_bytes=56 * 2**20
        ),
    )(codes, exps, text_bank)


def solution(mesh):
    return jax.shard_map(
        local,
        mesh=mesh,
        in_specs=(P(("dp", "bank"), None), P(("dp", "bank"), None), P("bank", None)),
        out_specs=P(("dp", "bank"), None),
        check_vma=False,
    )
```
